512 devices in a mesh: cent: 8 (over z), pts: 64 (over x, y, core).
Axes of the slice: x: 4, y: 8, z: 8, core: 2. Of those that a mesh axis runs over, the one named last changes fastest.
Arguments:
- points: bfloat16 [65536, 1024], P('pts'), may hold values from -120 to 120
- centroids: bfloat16 [4096, 1024], P(('cent', 'pts')), may hold values from -4 to 4
Outputs:
- new_centroids: bfloat16 [4096, 1024], P(('cent', 'pts'))
- lse: float32 [65536], P('pts')
The draws below stay inside these ranges and needn't reach their ends.
All inputs are finite; a program needn't handle non-finite values.
Results may differ from the reference program's by a relative error of at most 0.006.
Values may be sent and summed in bfloat16 or wider, within the bound.
No kernel may reach another device: no remote copies, remote signals or barrier semaphores. Data moves between devices by JAX's collectives and lax.ppermute only.
A program may use at most 64 MiB of HBM per device.

```python
import jax
import jax.numpy as jnp
from jax import lax

D = 1024
PT_DEV = 1024
K = 4096
N = 65536


def shared_table(key):
    return jnp.clip(jax.random.normal(key, (K, D), jnp.float32), -4.0, 4.0)


def draw_centroids(key, part):
    table = shared_table(key)
    return table.astype(jnp.bfloat16)


def draw_points(key, part):
    table = shared_table(key)
    key = jax.random.fold_in(key, 2)
    first = jax.random.fold_in(key, 0)
    third = jax.random.fold_in(key, 2)
    fourth = jax.random.fold_in(key, 3)
    values = jnp.clip(jax.random.normal(first, (N, D), jnp.float32), -6.0, 6.0)
    picks = jax.random.randint(third, (N,), 0, K)
    others = (picks + 1) % K
    level = jax.random.randint(fourth, (N,), 0, 3).astype(jnp.float32)
    strength = 1.0 + (120.0 + 40.0 * level) / D ** 0.5
    aligned = strength[:, None] * 0.5 * (table[picks] + table[others])
    chosen = jnp.arange(N) % 64 == 5
    values = jnp.where(chosen[:, None], aligned, values)
    return values.astype(jnp.bfloat16)


def setup_inputs(seed: int = 0) -> dict:
    key_list = jax.random.split(jax.random.key(seed), 3)
    points = draw_points(jax.random.fold_in(key_list[2], 71), 0)
    centroids = draw_centroids(jax.random.fold_in(key_list[2], 71), 0)
    return {"points": points, "centroids": centroids}


def reference(points, centroids):
    scale = 2.0 / (D ** 0.5)
    cent_f = centroids.astype(jnp.float32)
    sq_norms = jnp.sum(cent_f * cent_f, axis=1)
    blocks = points.reshape(N // PT_DEV, PT_DEV, D)

    def step(carry, block):
        logits = (jnp.dot(block, centroids.T, preferred_element_type=jnp.float32) - 0.5 * sq_norms[None, :]) * scale
        top = jnp.max(logits, axis=1)
        lse_rows = top + jnp.log(jnp.sum(jnp.exp(logits - top[:, None]), axis=1))
        resp = jnp.exp(logits - lse_rows[:, None]).astype(jnp.bfloat16)
        sums = carry[0] + jnp.dot(resp.T, block, preferred_element_type=jnp.float32)
        mass = carry[1] + jnp.sum(resp.astype(jnp.float32), axis=0)
        return (sums, mass), lse_rows

    init = (jnp.zeros((K, D), jnp.float32), jnp.zeros((K,), jnp.float32))
    (sums, mass), lse = lax.scan(step, init, blocks)
    new_centroids = ((sums + cent_f) / (mass[:, None] + 1.0)).astype(jnp.bfloat16)
    return new_centroids, lse.reshape(N)
```

```python
import functools
import math

import jax
import jax.numpy as jnp
from jax import lax
from jax.experimental import pallas as pl
from jax.experimental.pallas import tpu as pltpu
from jax.sharding import Mesh, PartitionSpec as P

LANES = 128
CORES = 2
VMEM_LIMIT = 40 * 1024 * 1024
F32 = jnp.float32
BF16 = jnp.bfloat16


def in_vmem(x):
    return pltpu.with_memory_space_constraint(x, pltpu.VMEM)


def whole(n):
    return [pl.BlockSpec(memory_space=pltpu.VMEM)] * n


def local_kernel(scale, core_ref, group_ref, own_ref, other_ref, logits_ref, part_ref):
    group = group_ref[...]
    group_f = group.astype(F32)
    half_norms = 0.5 * jnp.sum(group_f * group_f, axis=1, keepdims=True)
    core = core_ref[0]
    points = own_ref.shape[0]
    width = 2 * LANES
    for which, ref in enumerate((own_ref, other_ref)):
        rows = []
        for start in range(0, points, width):
            dots = lax.dot_general(
                group, ref[pl.ds(start, width), :], (((1,), (1,)), ((), ())), preferred_element_type=F32
            )
            logits = (dots - half_norms) * scale
            logits_ref[which, :, pl.ds(start, width)] = logits
            top = jnp.max(logits, axis=0, keepdims=True)
            lse = top + jnp.log(jnp.sum(jnp.exp(logits - top), axis=0, keepdims=True))
            rows += [lse[:, i : i + LANES] for i in range(0, width, LANES)]
        block = jnp.concatenate(rows, axis=0)
        count = block.shape[0]
        place = pl.multiple_of((core if which == 0 else 1 - core) * count, count)
        for peer in range(part_ref.shape[0]):
            part_ref[peer, pl.ds(place, count), :] = block


def sums_kernel(core_ref, logits_ref, parts_ref, own_ref, other_ref, send_ref, lse_ref, resp_ref, total_ref):
    parts = parts_ref[...]
    top = jnp.max(parts, axis=0)
    total_ref[...] = top + jnp.log(jnp.sum(jnp.exp(parts - top[None]), axis=0))
    core = core_ref[0]
    points, width = own_ref.shape
    count = points // LANES
    mass = jnp.zeros((logits_ref.shape[1], LANES), F32)
    for which in range(CORES):
        place = pl.multiple_of((core if which == 0 else 1 - core) * count, count)
        lse = total_ref[pl.ds(place, count), :]
        if which == 0:
            lse_ref[...] = lse
        for i in range(count):
            cols = pl.ds(i * LANES, LANES)
            resp = jnp.exp(logits_ref[which, :, cols] - lse[i : i + 1, :]).astype(BF16)
            resp_ref[which, :, cols] = resp
            mass += resp.astype(F32)
    mass = jnp.sum(mass, axis=1, keepdims=True)
    high = mass.astype(BF16).astype(F32)
    lane = lax.broadcasted_iota(jnp.int32, (mass.shape[0], LANES), 1)
    send_ref[:, pl.ds(width, LANES)] = jnp.where(lane < LANES // 2, high, mass - high).astype(BF16)
    step = 2 * LANES
    for start in range(0, width, step):
        cols = pl.ds(start, step)
        sums = jnp.dot(resp_ref[0], own_ref[:, cols], preferred_element_type=F32)
        sums += jnp.dot(resp_ref[1], other_ref[:, cols], preferred_element_type=F32)
        send_ref[:, cols] = sums.astype(BF16)


def update_kernel(got_ref, cent_ref, out_ref):
    own, width = cent_ref.shape
    step = 2 * own
    total = got_ref[pl.ds(0, step), :].astype(F32)
    for start in range(step, got_ref.shape[0], step):
        total += got_ref[pl.ds(start, step), :].astype(F32)
    total = total[:own] + total[own:]
    mass = total[:, width : width + 1] + total[:, width + LANES // 2 : width + LANES // 2 + 1]
    out_ref[...] = ((total[:, :width] + cent_ref[...].astype(F32)) / (mass + 1.0)).astype(BF16)


def body(points, centroids):
    rows, width = points.shape
    own = centroids.shape[0]
    chips = lax.axis_size("chip")
    groups = lax.axis_size("cent") * CORES
    rank = own * chips
    params = pltpu.CompilerParams(vmem_limit_bytes=VMEM_LIMIT)
    smem = pl.BlockSpec(memory_space=pltpu.SMEM)
    core = lax.axis_index("core").astype(jnp.int32).reshape(1)

    other = lax.ppermute(points, "core", [(0, 1), (1, 0)])
    sent = jnp.broadcast_to(centroids[None], (chips, own, width))
    group = lax.all_to_all(sent, "chip", 0, 0).reshape(rank, width)

    logits, part = pl.pallas_call(
        functools.partial(local_kernel, 2.0 / math.sqrt(width)),
        out_shape=(
            pltpu.VMEM((CORES, rank, rows), F32),
            jax.ShapeDtypeStruct((groups, CORES * rows // LANES, LANES), F32),
        ),
        in_specs=[smem] + whole(3),
        out_specs=tuple(whole(2)),
        compiler_params=params,
        name="local",
    )(core, in_vmem(group), in_vmem(points), in_vmem(other))

    parts = lax.all_to_all(part, ("cent", "core"), 0, 0)

    send, lse = pl.pallas_call(
        sums_kernel,
        out_shape=(
            jax.ShapeDtypeStruct((rank, width + LANES), BF16),
            jax.ShapeDtypeStruct((rows // LANES, LANES), F32),
        ),
        in_specs=[smem] + whole(4),
        out_specs=tuple(whole(2)),
        scratch_shapes=[
            pltpu.VMEM((CORES, rank, rows), BF16),
            pltpu.VMEM((CORES * rows // LANES, LANES), F32),
        ],
        compiler_params=params,
        name="sums",
    )(core, in_vmem(logits), in_vmem(parts), in_vmem(points), in_vmem(other))

    got = lax.all_to_all(send.reshape(chips, own, width + LANES), "chip", 0, 0)

    updated = pl.pallas_call(
        update_kernel,
        out_shape=jax.ShapeDtypeStruct((own, width), BF16),
        in_specs=whole(2),
        out_specs=whole(1)[0],
        compiler_params=params,
        name="update",
    )(in_vmem(got.reshape(rank, width + LANES)), centroids)
    return updated, lse.reshape(rows)


def solution(mesh):
    cent, pts = mesh.shape["cent"], mesh.shape["pts"]
    fine = Mesh(mesh.devices.reshape(cent, pts // CORES, CORES), ("cent", "chip", "core"))
    spread = P(("cent", "chip", "core"), None)
    return jax.shard_map(
        body,
        mesh=fine,
        in_specs=(P(("chip", "core"), None), spread),
        out_specs=(spread, P(("chip", "core"))),
        check_vma=False,
    )
```

```python
import functools
import math

import jax
import jax.numpy as jnp
from jax import lax
from jax.experimental import pallas as pl
from jax.experimental.pallas import tpu as pltpu
from jax.sharding import Mesh, PartitionSpec as P

LANES = 128
CORES = 2
VMEM_LIMIT = 40 * 1024 * 1024
F32 = jnp.float32
BF16 = jnp.bfloat16


def in_vmem(x):
    return pltpu.with_memory_space_constraint(x, pltpu.VMEM)


def whole(n):
    return [pl.BlockSpec(memory_space=pltpu.VMEM)] * n


def local_kernel(scale, core_ref, group_ref, other_ref, from_ref, logits_ref, part_ref, own_ref, sems):
    step = own_ref.shape[0] // sems.shape[0]
    copies = []
    for i in range(sems.shape[0]):
        part = pl.ds(i * step, step)
        copies.append(pltpu.make_async_copy(from_ref.at[part, :], own_ref.at[part, :], sems.at[i]))
        copies[-1].start()
    core = core_ref[0]

    def half(which, ref):
        group = group_ref[...]
        group_f = group.astype(F32)
        half_norms = 0.5 * jnp.sum(group_f * group_f, axis=1, keepdims=True)
        width = 2 * LANES
        rows = []
        for start in range(0, ref.shape[0], width):
            dots = lax.dot_general(
                group, ref[pl.ds(start, width), :], (((1,), (1,)), ((), ())), preferred_element_type=F32
            )
            logits = (dots - half_norms) * scale
            logits_ref[which, :, pl.ds(start, width)] = logits
            top = jnp.max(logits, axis=0, keepdims=True)
            lse = top + jnp.log(jnp.sum(jnp.exp(logits - top), axis=0, keepdims=True))
            rows += [lse[:, i : i + LANES] for i in range(0, width, LANES)]
        block = jnp.concatenate(rows, axis=0)
        count = block.shape[0]
        place = pl.multiple_of((core if which == 0 else 1 - core) * count, count)
        for peer in range(part_ref.shape[0]):
            part_ref[peer, pl.ds(place, count), :] = block

    @pl.when(core >= 0)
    def _():
        half(1, other_ref)

    for copy in copies:
        copy.wait()

    @pl.when(core >= 0)
    def _():
        half(0, own_ref)


def sums_kernel(core_ref, logits_ref, parts_ref, own_ref, other_ref, send_ref, lse_ref, resp_ref, total_ref):
    parts = parts_ref[...]
    top = jnp.max(parts, axis=0)
    total_ref[...] = top + jnp.log(jnp.sum(jnp.exp(parts - top[None]), axis=0))
    core = core_ref[0]
    points, width = own_ref.shape
    count = points // LANES
    mass = jnp.zeros((logits_ref.shape[1], LANES), F32)
    for which in range(CORES):
        place = pl.multiple_of((core if which == 0 else 1 - core) * count, count)
        lse = total_ref[pl.ds(place, count), :]
        if which == 0:
            lse_ref[...] = lse
        for i in range(count):
            cols = pl.ds(i * LANES, LANES)
            resp = jnp.exp(logits_ref[which, :, cols] - lse[i : i + 1, :]).astype(BF16)
            resp_ref[which, :, cols] = resp
            mass += resp.astype(F32)
    mass = jnp.sum(mass, axis=1, keepdims=True)
    high = mass.astype(BF16).astype(F32)
    lane = lax.broadcasted_iota(jnp.int32, (mass.shape[0], LANES), 1)
    send_ref[:, pl.ds(width, LANES)] = jnp.where(lane < LANES // 2, high, mass - high).astype(BF16)
    step = 2 * LANES
    for start in range(0, width, step):
        cols = pl.ds(start, step)
        sums = jnp.dot(resp_ref[0], own_ref[:, cols], preferred_element_type=F32)
        sums += jnp.dot(resp_ref[1], other_ref[:, cols], preferred_element_type=F32)
        send_ref[:, cols] = sums.astype(BF16)


def update_kernel(got_ref, cent_ref, out_ref):
    own, width = cent_ref.shape
    step = 2 * own
    total = got_ref[pl.ds(0, step), :].astype(F32)
    for start in range(step, got_ref.shape[0], step):
        total += got_ref[pl.ds(start, step), :].astype(F32)
    total = total[:own] + total[own:]
    mass = total[:, width : width + 1] + total[:, width + LANES // 2 : width + LANES // 2 + 1]
    out_ref[...] = ((total[:, :width] + cent_ref[...].astype(F32)) / (mass + 1.0)).astype(BF16)


def body(points, centroids):
    rows, width = points.shape
    own = centroids.shape[0]
    chips = lax.axis_size("chip")
    groups = lax.axis_size("cent") * CORES
    rank = own * chips
    params = pltpu.CompilerParams(vmem_limit_bytes=VMEM_LIMIT)
    smem = pl.BlockSpec(memory_space=pltpu.SMEM)
    core = lax.axis_index("core").astype(jnp.int32).reshape(1)

    other = lax.ppermute(points, "core", [(0, 1), (1, 0)])
    sent, core = lax.optimization_barrier((jnp.broadcast_to(centroids[None], (chips, own, width)), core))
    group = lax.all_to_all(sent, "chip", 0, 0).reshape(rank, width)

    logits, part, points = pl.pallas_call(
        functools.partial(local_kernel, 2.0 / math.sqrt(width)),
        out_shape=(
            pltpu.VMEM((CORES, rank, rows), F32),
            jax.ShapeDtypeStruct((groups, CORES * rows // LANES, LANES), F32),
            pltpu.VMEM((rows, width), BF16),
        ),
        in_specs=[smem] + whole(2) + [pl.BlockSpec(memory_space=pl.ANY)],
        out_specs=tuple(whole(3)),
        scratch_shapes=[pltpu.SemaphoreType.DMA((4,))],
        compiler_params=params,
        name="local",
    )(core, in_vmem(group), in_vmem(other), pltpu.with_memory_space_constraint(points, pltpu.HBM))

    parts = lax.all_to_all(part, ("cent", "core"), 0, 0)

    send, lse = pl.pallas_call(
        sums_kernel,
        out_shape=(
            jax.ShapeDtypeStruct((rank, width + LANES), BF16),
            jax.ShapeDtypeStruct((rows // LANES, LANES), F32),
        ),
        in_specs=[smem] + whole(4),
        out_specs=tuple(whole(2)),
        scratch_shapes=[
            pltpu.VMEM((CORES, rank, rows), BF16),
            pltpu.VMEM((CORES * rows // LANES, LANES), F32),
        ],
        compiler_params=params,
        name="sums",
    )(core, in_vmem(logits), in_vmem(parts), in_vmem(points), in_vmem(other))

    got = lax.all_to_all(send.reshape(chips, own, width + LANES), "chip", 0, 0)

    updated = pl.pallas_call(
        update_kernel,
        out_shape=jax.ShapeDtypeStruct((own, width), BF16),
        in_specs=whole(2),
        out_specs=whole(1)[0],
        compiler_params=params,
        name="update",
    )(in_vmem(got.reshape(rank, width + LANES)), centroids)
    return updated, lse.reshape(rows)


def solution(mesh):
    cent, pts = mesh.shape["cent"], mesh.shape["pts"]
    fine = Mesh(mesh.devices.reshape(cent, pts // CORES, CORES), ("cent", "chip", "core"))
    spread = P(("cent", "chip", "core"), None)
    return jax.shard_map(
        body,
        mesh=fine,
        in_specs=(P(("chip", "core"), None), spread),
        out_specs=(spread, P(("chip", "core"))),
        check_vma=False,
    )
```

```python
import functools
import math

import jax
import jax.numpy as jnp
from jax import lax
from jax.experimental import pallas as pl
from jax.experimental.pallas import tpu as pltpu
from jax.sharding import Mesh, PartitionSpec as P

LANES = 128
CORES = 2
ACROSS = 4
PIECES = 4
STAGE_FLOPS = 10**10
VMEM_LIMIT = 40 * 1024 * 1024
F32 = jnp.float32
BF16 = jnp.bfloat16


def in_vmem(x):
    return pltpu.with_memory_space_constraint(x, pltpu.VMEM)


def whole(n):
    return [pl.BlockSpec(memory_space=pltpu.VMEM)] * n


def stage_kernel(points_ref, *refs):
    *out_refs, sems = refs
    copies, place = [], 0
    for i, ref in enumerate(out_refs):
        copies.append(pltpu.make_async_copy(points_ref.at[pl.ds(place, ref.shape[0]), :], ref, sems.at[i]))
        copies[-1].start()
        place += ref.shape[0]
    for copy in copies:
        copy.wait()


def local_kernel(scale, core_ref, group_ref, *refs):
    own_refs, from_refs = refs[:PIECES], refs[PIECES : 2 * PIECES]
    logits_ref, part_ref, other_ref, held_ref, sems = refs[2 * PIECES :]
    copies, place = [], 0
    for i, ref in enumerate(from_refs):
        copies.append(pltpu.make_async_copy(ref, other_ref.at[pl.ds(place, ref.shape[0]), :], sems.at[i]))
        copies[-1].start()
        place += ref.shape[0]
    core = core_ref[0]

    def block_of(which, pieces, skip):
        group = group_ref[...]
        group_f = group.astype(F32)
        half_norms = 0.5 * jnp.sum(group_f * group_f, axis=1, keepdims=True)
        width = 2 * LANES
        rows = []
        start = skip
        for ref in pieces:
            for first in range(0, ref.shape[0], width):
                dots = lax.dot_general(
                    group, ref[pl.ds(first, width), :], (((1,), (1,)), ((), ())), preferred_element_type=F32
                )
                logits = (dots - half_norms) * scale
                logits_ref[which, :, pl.ds(start, width)] = logits
                top = jnp.max(logits, axis=0, keepdims=True)
                lse = top + jnp.log(jnp.sum(jnp.exp(logits - top), axis=0, keepdims=True))
                rows += [lse[:, i : i + LANES] for i in range(0, width, LANES)]
                start += width
        return jnp.concatenate(rows, axis=0)

    def spread(which, block):
        count = block.shape[0]
        place = pl.multiple_of((core if which == 0 else 1 - core) * count, count)
        for peer in range(part_ref.shape[0]):
            part_ref[peer, pl.ds(place, count), :] = block

    rows = other_ref.shape[0] // 2
    first, second = copies[: PIECES // 2], copies[PIECES // 2 :]

    @pl.when(core >= 0)
    def _():
        spread(0, block_of(0, own_refs, 0))

    for copy in first:
        copy.wait()

    @pl.when(core >= 0)
    def _():
        held_ref[...] = block_of(1, [other_ref.at[pl.ds(0, rows), :]], 0)

    for copy in second:
        copy.wait()

    @pl.when(core >= 0)
    def _():
        late = block_of(1, [other_ref.at[pl.ds(rows, rows), :]], rows)
        spread(1, jnp.concatenate([held_ref[...], late], axis=0))


def sums_kernel(core_ref, logits_ref, parts_ref, *refs):
    own_refs, (other_ref, send_ref, lse_ref, resp_ref, total_ref) = refs[:PIECES], refs[PIECES:]
    parts = parts_ref[...]
    top = jnp.max(parts, axis=0)
    total_ref[...] = top + jnp.log(jnp.sum(jnp.exp(parts - top[None]), axis=0))
    core = core_ref[0]
    points, width = other_ref.shape
    count = points // LANES
    mass = jnp.zeros((logits_ref.shape[1], LANES), F32)
    for which in range(CORES):
        place = pl.multiple_of((core if which == 0 else 1 - core) * count, count)
        lse = total_ref[pl.ds(place, count), :]
        if which == 0:
            lse_ref[...] = lse
        for i in range(count):
            cols = pl.ds(i * LANES, LANES)
            resp = jnp.exp(logits_ref[which, :, cols] - lse[i : i + 1, :]).astype(BF16)
            resp_ref[which, :, cols] = resp
            mass += resp.astype(F32)
    mass = jnp.sum(mass, axis=1, keepdims=True)
    high = mass.astype(BF16).astype(F32)
    lane = lax.broadcasted_iota(jnp.int32, (mass.shape[0], LANES), 1)
    send_ref[:, pl.ds(width, LANES)] = jnp.where(lane < LANES // 2, high, mass - high).astype(BF16)
    step = 2 * LANES
    for start in range(0, width, step):
        cols = pl.ds(start, step)
        sums = jnp.dot(resp_ref[1], other_ref[:, cols], preferred_element_type=F32)
        first = 0
        for ref in own_refs:
            part = pl.ds(first, ref.shape[0])
            sums += jnp.dot(resp_ref[0, :, part], ref[:, cols], preferred_element_type=F32)
            first += ref.shape[0]
        send_ref[:, cols] = sums.astype(BF16)


def update_kernel(got_ref, cent_ref, out_ref):
    own, width = cent_ref.shape
    step = 2 * own
    total = got_ref[pl.ds(0, step), :].astype(F32)
    for start in range(step, got_ref.shape[0], step):
        total += got_ref[pl.ds(start, step), :].astype(F32)
    total = total[:own] + total[own:]
    mass = total[:, width : width + 1] + total[:, width + LANES // 2 : width + LANES // 2 + 1]
    out_ref[...] = ((total[:, :width] + cent_ref[...].astype(F32)) / (mass + 1.0)).astype(BF16)


def body(points, centroids):
    rows, width = points.shape
    own = centroids.shape[0]
    chips = lax.axis_size("chip")
    groups = lax.axis_size("cent") * CORES
    rank = own * chips
    along = chips // ACROSS
    order = [[(x + y) % ACROSS * along + y for x in range(ACROSS) for y in range(along)]]
    params = pltpu.CompilerParams(vmem_limit_bytes=VMEM_LIMIT)
    smem = pl.BlockSpec(memory_space=pltpu.SMEM)
    core = lax.axis_index("core").astype(jnp.int32).reshape(1)

    sent = jnp.broadcast_to(centroids[None], (chips, own, width))
    sent, points = lax.optimization_barrier((sent, points))
    group = lax.all_to_all(sent, "chip", 0, 0, axis_index_groups=order).reshape(rank, width)

    mine = pl.pallas_call(
        stage_kernel,
        out_shape=[pltpu.VMEM((rows // PIECES, width), BF16)] * PIECES,
        in_specs=[pl.BlockSpec(memory_space=pl.ANY)],
        out_specs=whole(PIECES),
        scratch_shapes=[pltpu.SemaphoreType.DMA((PIECES,))],
        compiler_params=params,
        cost_estimate=pl.CostEstimate(flops=STAGE_FLOPS, transcendentals=0, bytes_accessed=4 * rows * width),
        name="stage",
    )(pltpu.with_memory_space_constraint(points, pltpu.HBM))
    mine = [in_vmem(x) for x in mine]
    theirs = [lax.ppermute(x, "core", [(0, 1), (1, 0)]) for x in mine]

    logits, part, other = pl.pallas_call(
        functools.partial(local_kernel, 2.0 / math.sqrt(width)),
        out_shape=(
            pltpu.VMEM((CORES, rank, rows), F32),
            jax.ShapeDtypeStruct((groups, CORES * rows // LANES, LANES), F32),
            pltpu.VMEM((rows, width), BF16),
        ),
        in_specs=[smem] + whole(1 + PIECES) + [pl.BlockSpec(memory_space=pl.ANY)] * PIECES,
        out_specs=tuple(whole(3)),
        scratch_shapes=[pltpu.VMEM((rows // 2 // LANES, LANES), F32), pltpu.SemaphoreType.DMA((PIECES,))],
        compiler_params=params,
        name="local",
    )(core, in_vmem(group), *mine, *theirs)

    parts = lax.all_to_all(part, ("core", "cent"), 0, 0)

    send, lse = pl.pallas_call(
        sums_kernel,
        out_shape=(
            jax.ShapeDtypeStruct((rank, width + LANES), BF16),
            jax.ShapeDtypeStruct((rows // LANES, LANES), F32),
        ),
        in_specs=[smem] + whole(3 + PIECES),
        out_specs=tuple(whole(2)),
        scratch_shapes=[
            pltpu.VMEM((CORES, rank, rows), BF16),
            pltpu.VMEM((CORES * rows // LANES, LANES), F32),
        ],
        compiler_params=params,
        name="sums",
    )(core, in_vmem(logits), in_vmem(parts), *mine, in_vmem(other))

    got = lax.all_to_all(send.reshape(chips, own, width + LANES), "chip", 0, 0, axis_index_groups=order)

    updated = pl.pallas_call(
        update_kernel,
        out_shape=jax.ShapeDtypeStruct((own, width), BF16),
        in_specs=whole(2),
        out_specs=whole(1)[0],
        compiler_params=params,
        name="update",
    )(in_vmem(got.reshape(rank, width + LANES)), centroids)
    return updated, lse.reshape(rows)


def solution(mesh):
    cent, pts = mesh.shape["cent"], mesh.shape["pts"]
    fine = Mesh(mesh.devices.reshape(cent, pts // CORES, CORES), ("cent", "chip", "core"))
    spread = P(("cent", "chip", "core"), None)
    return jax.shard_map(
        body,
        mesh=fine,
        in_specs=(P(("chip", "core"), None), spread),
        out_specs=(spread, P(("chip", "core"))),
        check_vma=False,
    )
```

```python
import functools
import math

import jax
import jax.numpy as jnp
from jax import lax
from jax.experimental import pallas as pl
from jax.experimental.pallas import tpu as pltpu
from jax.sharding import Mesh, PartitionSpec as P

LANES = 128
CORES = 2
ACROSS = 4
PIECES = 4
STAGE_FLOPS = 10**10
VMEM_LIMIT = 40 * 1024 * 1024
F32 = jnp.float32
BF16 = jnp.bfloat16


def in_vmem(x):
    return pltpu.with_memory_space_constraint(x, pltpu.VMEM)


def whole(n):
    return [pl.BlockSpec(memory_space=pltpu.VMEM)] * n


def stage_kernel(points_ref, *refs):
    *out_refs, sems = refs
    copies, place = [], 0
    for i, ref in enumerate(out_refs):
        copies.append(pltpu.make_async_copy(points_ref.at[pl.ds(place, ref.shape[0]), :], ref, sems.at[i]))
        copies[-1].start()
        place += ref.shape[0]
    for copy in copies:
        copy.wait()


def local_kernel(scale, core_ref, group_ref, *refs):
    own_refs, from_refs = refs[:PIECES], refs[PIECES : 2 * PIECES]
    logits_ref, part_ref, other_ref, held_ref, sems = refs[2 * PIECES :]
    copies, place = [], 0
    for i, ref in enumerate(from_refs):
        copies.append(pltpu.make_async_copy(ref, other_ref.at[pl.ds(place, ref.shape[0]), :], sems.at[i]))
        copies[-1].start()
        place += ref.shape[0]
    core = core_ref[0]

    def block_of(which, pieces, skip):
        group = group_ref[...]
        group_f = group.astype(F32)
        half_norms = 0.5 * jnp.sum(group_f * group_f, axis=1, keepdims=True)
        width = 2 * LANES
        rows = []
        start = skip
        for ref in pieces:
            for first in range(0, ref.shape[0], width):
                dots = lax.dot_general(
                    group, ref[pl.ds(first, width), :], (((1,), (1,)), ((), ())), preferred_element_type=F32
                )
                logits = (dots - half_norms) * scale
                logits_ref[which, :, pl.ds(start, width)] = logits
                top = jnp.max(logits, axis=0, keepdims=True)
                lse = top + jnp.log(jnp.sum(jnp.exp(logits - top), axis=0, keepdims=True))
                rows += [lse[:, i : i + LANES] for i in range(0, width, LANES)]
                start += width
        return jnp.concatenate(rows, axis=0)

    def spread(which, block):
        count = block.shape[0]
        place = pl.multiple_of((core if which == 0 else 1 - core) * count, count)
        for peer in range(part_ref.shape[0]):
            part_ref[peer, pl.ds(place, count), :] = block

    rows = other_ref.shape[0] // 2
    first, second = copies[: PIECES // 2], copies[PIECES // 2 :]

    @pl.when(core >= 0)
    def _():
        spread(0, block_of(0, own_refs, 0))

    for copy in first:
        copy.wait()

    @pl.when(core >= 0)
    def _():
        held_ref[...] = block_of(1, [other_ref.at[pl.ds(0, rows), :]], 0)

    for copy in second:
        copy.wait()

    @pl.when(core >= 0)
    def _():
        late = block_of(1, [other_ref.at[pl.ds(rows, rows), :]], rows)
        spread(1, jnp.concatenate([held_ref[...], late], axis=0))


def sums_kernel(core_ref, logits_ref, parts_ref, *refs):
    own_refs, (other_ref, send_ref, lse_ref, resp_ref, total_ref) = refs[:PIECES], refs[PIECES:]
    parts = parts_ref[...]
    top = jnp.max(parts, axis=0)
    total_ref[...] = top + jnp.log(jnp.sum(jnp.exp(parts - top[None]), axis=0))
    core = core_ref[0]
    points, width = other_ref.shape
    count = points // LANES
    mass = jnp.zeros((logits_ref.shape[1], LANES), F32)
    for which in range(CORES):
        place = pl.multiple_of((core if which == 0 else 1 - core) * count, count)
        lse = total_ref[pl.ds(place, count), :]
        if which == 0:
            lse_ref[...] = lse
        for i in range(count):
            cols = pl.ds(i * LANES, LANES)
            resp = jnp.exp(logits_ref[which, :, cols] - lse[i : i + 1, :]).astype(BF16)
            resp_ref[which, :, cols] = resp
            mass += resp.astype(F32)
    mass = jnp.sum(mass, axis=1, keepdims=True)
    high = mass.astype(BF16).astype(F32)
    lane = lax.broadcasted_iota(jnp.int32, (mass.shape[0], LANES), 1)
    send_ref[:, pl.ds(width, LANES)] = jnp.where(lane < LANES // 2, high, mass - high).astype(BF16)
    step = 2 * LANES
    for start in range(0, width, step):
        cols = pl.ds(start, step)
        sums = jnp.dot(resp_ref[1], other_ref[:, cols], preferred_element_type=F32)
        first = 0
        for ref in own_refs:
            part = pl.ds(first, ref.shape[0])
            sums += jnp.dot(resp_ref[0, :, part], ref[:, cols], preferred_element_type=F32)
            first += ref.shape[0]
        send_ref[:, cols] = sums.astype(BF16)


def update_kernel(got_ref, cent_ref, out_ref):
    own, width = cent_ref.shape
    step = 2 * own
    total = got_ref[pl.ds(0, step), :].astype(F32)
    for start in range(step, got_ref.shape[0], step):
        total += got_ref[pl.ds(start, step), :].astype(F32)
    total = total[:own] + total[own:]
    mass = total[:, width : width + 1] + total[:, width + LANES // 2 : width + LANES // 2 + 1]
    out_ref[...] = ((total[:, :width] + cent_ref[...].astype(F32)) / (mass + 1.0)).astype(BF16)


def body(points, centroids):
    rows, width = points.shape
    own = centroids.shape[0]
    chips = lax.axis_size("chip")
    groups = lax.axis_size("cent") * CORES
    rank = own * chips
    along = chips // ACROSS
    line = [x * along + (y + 2 * x) % along for y in range(along) for x in range(ACROSS)]
    order = [[CORES * k for k in line], [CORES * k + 1 for k in reversed(line)]]
    params = pltpu.CompilerParams(vmem_limit_bytes=VMEM_LIMIT)
    smem = pl.BlockSpec(memory_space=pltpu.SMEM)
    core = lax.axis_index("core").astype(jnp.int32).reshape(1)

    sent = jnp.broadcast_to(centroids[None], (chips, own, width))
    sent, points = lax.optimization_barrier((sent, points))
    group = lax.all_to_all(sent, ("chip", "core"), 0, 0, axis_index_groups=order).reshape(rank, width)

    mine = pl.pallas_call(
        stage_kernel,
        out_shape=[pltpu.VMEM((rows // PIECES, width), BF16)] * PIECES,
        in_specs=[pl.BlockSpec(memory_space=pl.ANY)],
        out_specs=whole(PIECES),
        scratch_shapes=[pltpu.SemaphoreType.DMA((PIECES,))],
        compiler_params=params,
        cost_estimate=pl.CostEstimate(flops=STAGE_FLOPS, transcendentals=0, bytes_accessed=4 * rows * width),
        name="stage",
    )(pltpu.with_memory_space_constraint(points, pltpu.HBM))
    mine = [in_vmem(x) for x in mine]
    theirs = [lax.ppermute(x, "core", [(0, 1), (1, 0)]) for x in mine]

    logits, part, other = pl.pallas_call(
        functools.partial(local_kernel, 2.0 / math.sqrt(width)),
        out_shape=(
            pltpu.VMEM((CORES, rank, rows), F32),
            jax.ShapeDtypeStruct((groups, CORES * rows // LANES, LANES), F32),
            pltpu.VMEM((rows, width), BF16),
        ),
        in_specs=[smem] + whole(1 + PIECES) + [pl.BlockSpec(memory_space=pl.ANY)] * PIECES,
        out_specs=tuple(whole(3)),
        scratch_shapes=[pltpu.VMEM((rows // 2 // LANES, LANES), F32), pltpu.SemaphoreType.DMA((PIECES,))],
        compiler_params=params,
        name="local",
    )(core, in_vmem(group), *mine, *theirs)

    parts = lax.all_to_all(part, ("core", "cent"), 0, 0)

    send, lse = pl.pallas_call(
        sums_kernel,
        out_shape=(
            jax.ShapeDtypeStruct((rank, width + LANES), BF16),
            jax.ShapeDtypeStruct((rows // LANES, LANES), F32),
        ),
        in_specs=[smem] + whole(3 + PIECES),
        out_specs=tuple(whole(2)),
        scratch_shapes=[
            pltpu.VMEM((CORES, rank, rows), BF16),
            pltpu.VMEM((CORES * rows // LANES, LANES), F32),
        ],
        compiler_params=params,
        name="sums",
    )(core, in_vmem(logits), in_vmem(parts), *mine, in_vmem(other))

    got = lax.all_to_all(send.reshape(chips, own, width + LANES), ("chip", "core"), 0, 0, axis_index_groups=order)

    updated = pl.pallas_call(
        update_kernel,
        out_shape=jax.ShapeDtypeStruct((own, width), BF16),
        in_specs=whole(2),
        out_specs=whole(1)[0],
        compiler_params=params,
        name="update",
    )(in_vmem(got.reshape(rank, width + LANES)), centroids)
    return updated, lse.reshape(rows)


def solution(mesh):
    cent, pts = mesh.shape["cent"], mesh.shape["pts"]
    fine = Mesh(mesh.devices.reshape(cent, pts // CORES, CORES), ("cent", "chip", "core"))
    spread = P(("cent", "chip", "core"), None)
    return jax.shard_map(
        body,
        mesh=fine,
        in_specs=(P(("chip", "core"), None), spread),
        out_specs=(spread, P(("chip", "core"))),
        check_vma=False,
    )
```

```python
import functools
import math

import jax
import jax.numpy as jnp
from jax import lax
from jax.experimental import pallas as pl
from jax.experimental.pallas import tpu as pltpu
from jax.sharding import Mesh, PartitionSpec as P

LANES = 128
CORES = 2
ACROSS = 4
PIECES = 4
STAGE_FLOPS = 10**10
VMEM_LIMIT = 40 * 1024 * 1024
F32 = jnp.float32
BF16 = jnp.bfloat16


def in_vmem(x):
    return pltpu.with_memory_space_constraint(x, pltpu.VMEM)


def whole(n):
    return [pl.BlockSpec(memory_space=pltpu.VMEM)] * n


def stage_kernel(points_ref, *refs):
    *out_refs, sems = refs
    copies, place = [], 0
    for i, ref in enumerate(out_refs):
        copies.append(pltpu.make_async_copy(points_ref.at[pl.ds(place, ref.shape[0]), :], ref, sems.at[i]))
        copies[-1].start()
        place += ref.shape[0]
    for copy in copies:
        copy.wait()


def local_kernel(scale, core_ref, group_ref, *refs):
    own_refs, near_ref, from_refs = refs[:PIECES], refs[PIECES], refs[PIECES + 1 : 2 * PIECES]
    logits_ref, part_ref, other_ref, held_ref, sems = refs[2 * PIECES :]
    copies, place = [], 0
    for i, ref in enumerate(from_refs):
        copies.append(pltpu.make_async_copy(ref, other_ref.at[pl.ds(place, ref.shape[0]), :], sems.at[i]))
        copies[-1].start()
        place += ref.shape[0]
    core = core_ref[0]

    def block_of(which, pieces, skip):
        group = group_ref[...]
        group_f = group.astype(F32)
        half_norms = 0.5 * jnp.sum(group_f * group_f, axis=1, keepdims=True)
        width = 2 * LANES
        rows = []
        start = skip
        for ref in pieces:
            for first in range(0, ref.shape[0], width):
                dots = lax.dot_general(
                    group, ref[pl.ds(first, width), :], (((1,), (1,)), ((), ())), preferred_element_type=F32
                )
                logits = (dots - half_norms) * scale
                logits_ref[which, :, pl.ds(start, width)] = logits
                top = jnp.max(logits, axis=0, keepdims=True)
                lse = top + jnp.log(jnp.sum(jnp.exp(logits - top), axis=0, keepdims=True))
                rows += [lse[:, i : i + LANES] for i in range(0, width, LANES)]
                start += width
        return jnp.concatenate(rows, axis=0)

    def spread(which, block):
        count = block.shape[0]
        place = pl.multiple_of((core if which == 0 else 1 - core) * count, count)
        for peer in range(part_ref.shape[0]):
            part_ref[peer, pl.ds(place, count), :] = block

    @pl.when(core >= 0)
    def _():
        spread(0, block_of(0, own_refs, 0))
        held_ref[...] = block_of(1, [near_ref], other_ref.shape[0])

    for copy in copies:
        copy.wait()

    @pl.when(core >= 0)
    def _():
        spread(1, jnp.concatenate([block_of(1, [other_ref], 0), held_ref[...]], axis=0))


def sums_kernel(core_ref, logits_ref, parts_ref, *refs):
    own_refs, near_ref = refs[:PIECES], refs[PIECES]
    other_ref, send_ref, lse_ref, resp_ref, total_ref = refs[PIECES + 1 :]
    parts = parts_ref[...]
    top = jnp.max(parts, axis=0)
    total_ref[...] = top + jnp.log(jnp.sum(jnp.exp(parts - top[None]), axis=0))
    core = core_ref[0]
    points, width = resp_ref.shape[2], other_ref.shape[1]
    far = other_ref.shape[0]
    count = points // LANES
    mass = jnp.zeros((logits_ref.shape[1], LANES), F32)
    for which in range(CORES):
        place = pl.multiple_of((core if which == 0 else 1 - core) * count, count)
        lse = total_ref[pl.ds(place, count), :]
        if which == 0:
            lse_ref[...] = lse
        for i in range(count):
            cols = pl.ds(i * LANES, LANES)
            resp = jnp.exp(logits_ref[which, :, cols] - lse[i : i + 1, :]).astype(BF16)
            resp_ref[which, :, cols] = resp
            mass += resp.astype(F32)
    mass = jnp.sum(mass, axis=1, keepdims=True)
    high = mass.astype(BF16).astype(F32)
    lane = lax.broadcasted_iota(jnp.int32, (mass.shape[0], LANES), 1)
    send_ref[:, pl.ds(width, LANES)] = jnp.where(lane < LANES // 2, high, mass - high).astype(BF16)
    step = 2 * LANES
    for start in range(0, width, step):
        cols = pl.ds(start, step)
        sums = jnp.dot(resp_ref[1, :, pl.ds(0, far)], other_ref[:, cols], preferred_element_type=F32)
        sums += jnp.dot(resp_ref[1, :, pl.ds(far, points - far)], near_ref[:, cols], preferred_element_type=F32)
        first = 0
        for ref in own_refs:
            part = pl.ds(first, ref.shape[0])
            sums += jnp.dot(resp_ref[0, :, part], ref[:, cols], preferred_element_type=F32)
            first += ref.shape[0]
        send_ref[:, cols] = sums.astype(BF16)


def update_kernel(got_ref, cent_ref, out_ref):
    own, width = cent_ref.shape
    step = 2 * own
    total = got_ref[pl.ds(0, step), :].astype(F32)
    for start in range(step, got_ref.shape[0], step):
        total += got_ref[pl.ds(start, step), :].astype(F32)
    total = total[:own] + total[own:]
    mass = total[:, width : width + 1] + total[:, width + LANES // 2 : width + LANES // 2 + 1]
    out_ref[...] = ((total[:, :width] + cent_ref[...].astype(F32)) / (mass + 1.0)).astype(BF16)


def body(points, centroids):
    rows, width = points.shape
    own = centroids.shape[0]
    chips = lax.axis_size("chip")
    groups = lax.axis_size("cent") * CORES
    rank = own * chips
    along = chips // ACROSS
    line = [x * along + (y + 2 * x) % along for y in range(along) for x in range(ACROSS)]
    order = [[CORES * k for k in line], [CORES * k + 1 for k in reversed(line)]]
    params = pltpu.CompilerParams(vmem_limit_bytes=VMEM_LIMIT)
    smem = pl.BlockSpec(memory_space=pltpu.SMEM)
    core = lax.axis_index("core").astype(jnp.int32).reshape(1)

    sent = jnp.broadcast_to(centroids[None], (chips, own, width))
    sent, points = lax.optimization_barrier((sent, points))
    group = lax.all_to_all(sent, ("chip", "core"), 0, 0, axis_index_groups=order).reshape(rank, width)

    mine = pl.pallas_call(
        stage_kernel,
        out_shape=[pltpu.VMEM((rows // PIECES, width), BF16)] * PIECES,
        in_specs=[pl.BlockSpec(memory_space=pl.ANY)],
        out_specs=whole(PIECES),
        scratch_shapes=[pltpu.SemaphoreType.DMA((PIECES,))],
        compiler_params=params,
        cost_estimate=pl.CostEstimate(flops=STAGE_FLOPS, transcendentals=0, bytes_accessed=4 * rows * width),
        name="stage",
    )(pltpu.with_memory_space_constraint(points, pltpu.HBM))
    mine = [in_vmem(x) for x in mine]
    theirs = [lax.ppermute(x, "core", [(0, 1), (1, 0)]) for x in mine]

    *theirs, near = theirs
    near = in_vmem(near)

    logits, part, other = pl.pallas_call(
        functools.partial(local_kernel, 2.0 / math.sqrt(width)),
        out_shape=(
            pltpu.VMEM((CORES, rank, rows), F32),
            jax.ShapeDtypeStruct((groups, CORES * rows // LANES, LANES), F32),
            pltpu.VMEM((rows - rows // PIECES, width), BF16),
        ),
        in_specs=[smem] + whole(2 + PIECES) + [pl.BlockSpec(memory_space=pl.ANY)] * (PIECES - 1),
        out_specs=tuple(whole(3)),
        scratch_shapes=[pltpu.VMEM((rows // PIECES // LANES, LANES), F32), pltpu.SemaphoreType.DMA((PIECES - 1,))],
        compiler_params=params,
        name="local",
    )(core, in_vmem(group), *mine, near, *theirs)

    parts = lax.all_to_all(part, ("core", "cent"), 0, 0)

    send, lse = pl.pallas_call(
        sums_kernel,
        out_shape=(
            jax.ShapeDtypeStruct((rank, width + LANES), BF16),
            jax.ShapeDtypeStruct((rows // LANES, LANES), F32),
        ),
        in_specs=[smem] + whole(4 + PIECES),
        out_specs=tuple(whole(2)),
        scratch_shapes=[
            pltpu.VMEM((CORES, rank, rows), BF16),
            pltpu.VMEM((CORES * rows // LANES, LANES), F32),
        ],
        compiler_params=params,
        name="sums",
    )(core, in_vmem(logits), in_vmem(parts), *mine, near, in_vmem(other))

    got = lax.all_to_all(send.reshape(chips, own, width + LANES), ("chip", "core"), 0, 0, axis_index_groups=order)

    updated = pl.pallas_call(
        update_kernel,
        out_shape=jax.ShapeDtypeStruct((own, width), BF16),
        in_specs=whole(2),
        out_specs=whole(1)[0],
        compiler_params=params,
        name="update",
    )(in_vmem(got.reshape(rank, width + LANES)), centroids)
    return updated, lse.reshape(rows)


def solution(mesh):
    cent, pts = mesh.shape["cent"], mesh.shape["pts"]
    fine = Mesh(mesh.devices.reshape(cent, pts // CORES, CORES), ("cent", "chip", "core"))
    spread = P(("cent", "chip", "core"), None)
    return jax.shard_map(
        body,
        mesh=fine,
        in_specs=(P(("chip", "core"), None), spread),
        out_specs=(spread, P(("chip", "core"))),
        check_vma=False,
    )
```

```python
import functools
import math

import jax
import jax.numpy as jnp
from jax import lax
from jax.experimental import pallas as pl
from jax.experimental.pallas import tpu as pltpu
from jax.sharding import Mesh, PartitionSpec as P

LANES = 128
CORES = 2
ACROSS = 4
PIECES = 4
STAGE_FLOPS = 10**10
VMEM_LIMIT = 40 * 1024 * 1024
F32 = jnp.float32
BF16 = jnp.bfloat16


def in_vmem(x):
    return pltpu.with_memory_space_constraint(x, pltpu.VMEM)


def whole(n):
    return [pl.BlockSpec(memory_space=pltpu.VMEM)] * n


def stage_kernel(points_ref, *refs):
    *out_refs, sems = refs
    copies, place = [], 0
    for i, ref in enumerate(out_refs):
        copies.append(pltpu.make_async_copy(points_ref.at[pl.ds(place, ref.shape[0]), :], ref, sems.at[i]))
        copies[-1].start()
        place += ref.shape[0]
    for copy in copies:
        copy.wait()


def local_kernel(scale, core_ref, group_ref, *refs):
    own_refs, near_ref, from_refs = refs[:PIECES], refs[PIECES], refs[PIECES + 1 : 2 * PIECES]
    logits_ref, part_ref, other_ref, held_ref, sems = refs[2 * PIECES :]
    copies, place = [], 0
    for i, ref in enumerate(from_refs):
        copies.append(pltpu.make_async_copy(ref, other_ref.at[pl.ds(place, ref.shape[0]), :], sems.at[i]))
        copies[-1].start()
        place += ref.shape[0]
    core = core_ref[0]

    def block_of(which, pieces, skip):
        group = group_ref[...]
        group_f = group.astype(F32)
        half_norms = 0.5 * jnp.sum(group_f * group_f, axis=1, keepdims=True)
        width = 2 * LANES
        rows = []
        start = skip
        for ref in pieces:
            for first in range(0, ref.shape[0], width):
                dots = lax.dot_general(
                    group, ref[pl.ds(first, width), :], (((1,), (1,)), ((), ())), preferred_element_type=F32
                )
                logits = (dots - half_norms) * scale
                logits_ref[which, :, pl.ds(start, width)] = logits
                top = jnp.max(logits, axis=0, keepdims=True)
                lse = top + jnp.log(jnp.sum(jnp.exp(logits - top), axis=0, keepdims=True))
                rows += [lse[:, i : i + LANES] for i in range(0, width, LANES)]
                start += width
        return jnp.concatenate(rows, axis=0)

    def spread(which, block):
        count = block.shape[0]
        place = pl.multiple_of((core if which == 0 else 1 - core) * count, count)
        for peer in range(part_ref.shape[0]):
            part_ref[peer, pl.ds(place, count), :] = block

    @pl.when(core >= 0)
    def _():
        spread(0, block_of(0, own_refs, 0))
        held_ref[...] = block_of(1, [near_ref], other_ref.shape[0])

    for copy in copies:
        copy.wait()

    @pl.when(core >= 0)
    def _():
        spread(1, jnp.concatenate([block_of(1, [other_ref], 0), held_ref[...]], axis=0))


def sums_kernel(core_ref, logits_ref, parts_ref, *refs):
    own_refs, near_ref = refs[:PIECES], refs[PIECES]
    other_ref, send_ref, lse_ref, resp_ref, total_ref = refs[PIECES + 1 :]
    parts = parts_ref[...]
    top = jnp.max(parts, axis=0)
    total_ref[...] = top + jnp.log(jnp.sum(jnp.exp(parts - top[None]), axis=0))
    core = core_ref[0]
    points, width = resp_ref.shape[2], other_ref.shape[1]
    far = other_ref.shape[0]
    count = points // LANES
    mass = jnp.zeros((logits_ref.shape[1], LANES), F32)
    for which in range(CORES):
        place = pl.multiple_of((core if which == 0 else 1 - core) * count, count)
        lse = total_ref[pl.ds(place, count), :]
        if which == 0:
            lse_ref[...] = lse
        for i in range(count):
            cols = pl.ds(i * LANES, LANES)
            resp = jnp.exp(logits_ref[which, :, cols] - lse[i : i + 1, :]).astype(BF16)
            resp_ref[which, :, cols] = resp
            mass += resp.astype(F32)
    mass = jnp.sum(mass, axis=1, keepdims=True)
    high = mass.astype(BF16).astype(F32)
    lane = lax.broadcasted_iota(jnp.int32, (mass.shape[0], LANES), 1)
    send_ref[:, pl.ds(width, LANES)] = jnp.where(lane < LANES // 2, high, mass - high).astype(BF16)
    step = 2 * LANES
    for start in range(0, width, step):
        cols = pl.ds(start, step)
        sums, first = 0.0, 0
        for ref in own_refs:
            part = pl.ds(first, ref.shape[0])
            sums += jnp.dot(resp_ref[0, :, part], ref[:, cols], preferred_element_type=F32)
            first += ref.shape[0]
        sums += jnp.dot(resp_ref[1, :, pl.ds(0, far)], other_ref[:, cols], preferred_element_type=F32)
        sums += jnp.dot(resp_ref[1, :, pl.ds(far, points - far)], near_ref[:, cols], preferred_element_type=F32)
        send_ref[:, cols] = sums.astype(BF16)


def update_kernel(got_ref, cent_ref, out_ref):
    own, width = cent_ref.shape
    step = 2 * own
    total = got_ref[pl.ds(0, step), :].astype(F32)
    for start in range(step, got_ref.shape[0], step):
        total += got_ref[pl.ds(start, step), :].astype(F32)
    total = total[:own] + total[own:]
    mass = total[:, width : width + 1] + total[:, width + LANES // 2 : width + LANES // 2 + 1]
    out_ref[...] = ((total[:, :width] + cent_ref[...].astype(F32)) / (mass + 1.0)).astype(BF16)


def body(points, centroids):
    rows, width = points.shape
    own = centroids.shape[0]
    chips = lax.axis_size("chip")
    groups = lax.axis_size("cent") * CORES
    rank = own * chips
    along = chips // ACROSS
    line = [x * along + (y + 2 * x) % along for y in range(along) for x in range(ACROSS)]
    order = [[CORES * k for k in line], [CORES * k + 1 for k in reversed(line)]]
    params = pltpu.CompilerParams(vmem_limit_bytes=VMEM_LIMIT)
    smem = pl.BlockSpec(memory_space=pltpu.SMEM)
    core = lax.axis_index("core").astype(jnp.int32).reshape(1)

    sent = jnp.broadcast_to(centroids[None], (chips, own, width))
    sent, points = lax.optimization_barrier((sent, points))
    group = lax.all_to_all(sent, ("chip", "core"), 0, 0, axis_index_groups=order).reshape(rank, width)

    mine = pl.pallas_call(
        stage_kernel,
        out_shape=[pltpu.VMEM((rows // PIECES, width), BF16)] * PIECES,
        in_specs=[pl.BlockSpec(memory_space=pl.ANY)],
        out_specs=whole(PIECES),
        scratch_shapes=[pltpu.SemaphoreType.DMA((PIECES,))],
        compiler_params=params,
        cost_estimate=pl.CostEstimate(flops=STAGE_FLOPS, transcendentals=0, bytes_accessed=4 * rows * width),
        name="stage",
    )(pltpu.with_memory_space_constraint(points, pltpu.HBM))
    mine = [in_vmem(x) for x in mine]
    theirs = [lax.ppermute(x, "core", [(0, 1), (1, 0)]) for x in mine]

    *theirs, near = theirs
    near = in_vmem(near)

    logits, part, other = pl.pallas_call(
        functools.partial(local_kernel, 2.0 / math.sqrt(width)),
        out_shape=(
            pltpu.VMEM((CORES, rank, rows), F32),
            jax.ShapeDtypeStruct((groups, CORES * rows // LANES, LANES), F32),
            pltpu.VMEM((rows - rows // PIECES, width), BF16),
        ),
        in_specs=[smem] + whole(2 + PIECES) + [pl.BlockSpec(memory_space=pl.ANY)] * (PIECES - 1),
        out_specs=tuple(whole(3)),
        scratch_shapes=[pltpu.VMEM((rows // PIECES // LANES, LANES), F32), pltpu.SemaphoreType.DMA((PIECES - 1,))],
        compiler_params=params,
        name="local",
    )(core, in_vmem(group), *mine, near, *theirs)

    parts = lax.all_to_all(part, ("core", "cent"), 0, 0)

    send, lse = pl.pallas_call(
        sums_kernel,
        out_shape=(
            jax.ShapeDtypeStruct((rank, width + LANES), BF16),
            jax.ShapeDtypeStruct((rows // LANES, LANES), F32),
        ),
        in_specs=[smem] + whole(4 + PIECES),
        out_specs=tuple(whole(2)),
        scratch_shapes=[
            pltpu.VMEM((CORES, rank, rows), BF16),
            pltpu.VMEM((CORES * rows // LANES, LANES), F32),
        ],
        compiler_params=params,
        name="sums",
    )(core, in_vmem(logits), in_vmem(parts), *mine, near, in_vmem(other))

    got = lax.all_to_all(send.reshape(chips, own, width + LANES), ("chip", "core"), 0, 0, axis_index_groups=order)

    updated = pl.pallas_call(
        update_kernel,
        out_shape=jax.ShapeDtypeStruct((own, width), BF16),
        in_specs=whole(2),
        out_specs=whole(1)[0],
        compiler_params=params,
        name="update",
    )(in_vmem(got.reshape(rank, width + LANES)), centroids)
    return updated, lse.reshape(rows)


def solution(mesh):
    cent, pts = mesh.shape["cent"], mesh.shape["pts"]
    fine = Mesh(mesh.devices.reshape(cent, pts // CORES, CORES), ("cent", "chip", "core"))
    spread = P(("cent", "chip", "core"), None)
    return jax.shard_map(
        body,
        mesh=fine,
        in_specs=(P(("chip", "core"), None), spread),
        out_specs=(spread, P(("chip", "core"))),
        check_vma=False,
    )
```
